256 devices in a mesh: row: 32 (over y, z_lo, core), feat: 8 (over z_hi, x).
Axes of the slice: x: 4, y: 4, z: 8 (z_hi: 2, z_lo: 4; z = z_hi * 4 + z_lo), core: 2. Of those that a mesh axis runs over, the one named last changes fastest.
Arguments:
- node_feats: bfloat16 [512, 32768], P('feat', 'row'), may hold values from -6 to 6
- self_weight: float32 [32768], P('row'), may hold values from 0.2 to 1
- hub_ids: int32 [512], P('row'), may hold values from 0 to 1023
- hub_adjacency: bfloat16 [512, 32768], P(None, 'row'), may hold values from -0.25 to 0.25
- send_blocks: int32 [32, 32, 4], P('row'), may hold values from 0 to 7
- recv_counts: int32 [32, 32], P('row'), may hold values from 0 to 4, as said below
- recv_targets: int32 [32, 32, 4], P('row'), may hold values from 0 to 7
- recv_tiles: bfloat16 [32, 32, 4, 128, 128], P('row'), may hold values from -0.125 to 0.125
- weight: bfloat16 [512, 512], replicated, may hold values from -0.25 to 0.25
- grad_out: bfloat16 [512, 32768], P('feat', 'row'), may hold values from -6 to 6
Outputs:
- activation: bfloat16 [512, 32768], P('feat', 'row')
- grad_in: bfloat16 [512, 32768], P('feat', 'row')
The draws below stay inside these ranges and needn't reach their ends.
Inputs may be any that keep to these rules, and one draw needn't show every extreme that they name: Reader d takes the first recv_counts[d, s] of the 4 slots from source s; some reader takes all 4 slots from every source. `send_blocks`: A block index within the source's nodes. `recv_targets`: A block index within the reader's nodes. `hub_ids`: A row within the owner's nodes; ids may repeat.
All inputs are finite; a program needn't handle non-finite values.
Results may differ from the reference program's by a relative error of at most 0.03.
Values may be sent and summed in bfloat16 or wider, within the bound.
No kernel may reach another device: no remote copies, remote signals or barrier semaphores. Data moves between devices by JAX's collectives and lax.ppermute only.
A program may use at most 64 MiB of HBM per device.

```python
import math
import jax
import jax.numpy as jnp
from jax import lax

H = 512
NODE_DEV = 1024
HUB_DEV = 16
SLOTS = 4
BLOCK = 128
NODES = 32768
HUBS = 512
N_ROW = 32


def draw_recv_counts(key, part):
    key = jax.random.fold_in(key, 11)
    key_base, key_heavy, key_pick = jax.random.split(key, 3)
    base = jax.random.randint(key_base, (N_ROW, N_ROW), 0, SLOTS + 1)
    heavy = jax.random.randint(key_heavy, (N_ROW,), 0, 4) == 0
    picked = jax.random.randint(key_pick, (), 0, N_ROW)
    heavy = jnp.logical_or(heavy, jnp.arange(N_ROW) == picked)
    return jnp.where(heavy[:, None], SLOTS, base).astype(jnp.int32)


def with_ends(array, own_key, least, top_value):
    index_at = [jax.random.randint(jax.random.fold_in(own_key, axis), (), 0, length) for axis, length in enumerate(array.shape)]
    longest = array.shape.index(max(array.shape))
    beside = index_at[:longest] + [(index_at[longest] + 1) % array.shape[longest]] + index_at[longest + 1:]
    return array.at[tuple(index_at)].set(least).at[tuple(beside)].set(top_value)


def shard_levels(rng, dims, pieces, low, top_value):
    loudness = 1.0
    for dim, parts in pieces:
        heights = jax.random.uniform(jax.random.fold_in(jax.random.fold_in(rng, 6), dim), (parts,), jnp.float32, low / len(pieces), top_value / len(pieces))
        loudness = loudness * jnp.repeat(jnp.exp(heights), dims[dim] // parts).reshape((-1,) + (1,) * (len(dims) - 1 - dim))
    return loudness


def noise(rng, extent, width, bound, pieces=(), held_as=jnp.bfloat16):
    array = jax.random.normal(rng, extent, jnp.float32) * width
    if len(pieces) > 0:
        array = shard_levels(rng, extent, pieces, -0.22, 0.18) * array
    return jnp.clip(array, min=-bound, max=bound).astype(held_as)


def setup_inputs(seed: int = 0) -> dict:
    key_list = jax.random.split(jax.random.key(seed), 11)
    node_feats = noise(key_list[0], (H, NODES), 1.0, 6.0, ((0, 8), (1, 32)))
    self_weight = jnp.clip(jnp.exp(math.log(1.0) - 1.609438 * jax.random.uniform(key_list[1], (NODES,), jnp.float32) ** shard_levels(key_list[1], (NODES,), ((0, 32),), -0.2, 0.2)), 0.2, 1.0)
    hub_ids = with_ends(jax.random.randint(key_list[2], (HUBS,), 0, NODE_DEV), jax.random.fold_in(key_list[2], 1), 0, NODE_DEV - 1).astype(jnp.int32)
    hub_adjacency = noise(key_list[3], (HUBS, NODES), HUBS ** -0.5, 0.25, ((1, 32),))
    send_blocks = with_ends(jax.random.randint(key_list[4], (N_ROW, N_ROW, SLOTS), 0, NODE_DEV // BLOCK), jax.random.fold_in(key_list[4], 1), 0, (NODE_DEV // BLOCK) - 1).astype(jnp.int32)
    recv_counts = draw_recv_counts(jax.random.fold_in(key_list[10], 71), 0)
    recv_targets = with_ends(jax.random.randint(key_list[6], (N_ROW, N_ROW, SLOTS), 0, NODE_DEV // BLOCK), jax.random.fold_in(key_list[6], 1), 0, (NODE_DEV // BLOCK) - 1).astype(jnp.int32)
    recv_tiles = noise(key_list[7], (N_ROW, N_ROW, SLOTS, BLOCK, BLOCK), (N_ROW * SLOTS * BLOCK * BLOCK // NODE_DEV) ** -0.5, 0.125, ((0, 32),))
    weight = noise(key_list[8], (H, H), H ** -0.5, 0.25)
    grad_out = noise(key_list[9], (H, NODES), 1.0, 6.0, ((0, 8), (1, 32)))
    return {"node_feats": node_feats, "self_weight": self_weight, "hub_ids": hub_ids, "hub_adjacency": hub_adjacency, "send_blocks": send_blocks, "recv_counts": recv_counts, "recv_targets": recv_targets, "recv_tiles": recv_tiles, "weight": weight, "grad_out": grad_out}


HIGH = lax.Precision.HIGHEST

def gelu_fn(values):
    return jax.nn.gelu(values, approximate=True)

def reference(node_feats, self_weight, hub_ids, hub_adjacency, send_blocks, recv_counts, recv_targets, recv_tiles, weight, grad_out):
    num_blocks = NODE_DEV // BLOCK
    feats_wide = node_feats.astype(jnp.float32)
    weight_wide = weight.astype(jnp.float32)
    adjacency_wide = hub_adjacency.astype(jnp.float32)
    owners = (jnp.arange(HUBS) // HUB_DEV).astype(jnp.int32)
    hub_nodes = (owners * NODE_DEV + hub_ids).astype(jnp.int32)
    hub_feats = jnp.take(feats_wide, hub_nodes, axis=1)
    hub_part = jnp.dot(hub_feats, adjacency_wide, precision=HIGH)
    blocks = feats_wide.reshape(H, N_ROW, num_blocks, BLOCK)
    sources = jnp.arange(N_ROW).astype(jnp.int32)[:, None]
    block_ids = jnp.arange(num_blocks).astype(jnp.int32)

    def live_of(reader):
        return (jnp.arange(SLOTS).astype(jnp.int32)[None, :] < recv_counts[reader][:, None]).astype(jnp.float32)

    def reader_sum(reader):
        chosen = send_blocks[:, reader, :]
        sent = blocks[:, sources, chosen, :]
        products = jnp.einsum('fski,skij->skfj', sent, recv_tiles[reader].astype(jnp.float32), precision=HIGH)
        place_into = (recv_targets[reader][:, :, None] == block_ids[None, None, :]).astype(jnp.float32) * live_of(reader)[:, :, None]
        gathered = jnp.einsum('skfj,skb->fbj', products, place_into, precision=HIGH)
        return gathered.reshape(H, NODE_DEV)
    rem_part = lax.map(reader_sum, jnp.arange(N_ROW).astype(jnp.int32))
    rem_part = jnp.transpose(rem_part, (1, 0, 2)).reshape(H, NODES)
    aggregated = (self_weight[None, :] * feats_wide + hub_part + rem_part).astype(jnp.bfloat16)
    pre = jnp.dot(weight_wide.T, aggregated.astype(jnp.float32), precision=HIGH)
    activation = gelu_fn(pre).astype(jnp.bfloat16)
    _, pullback = jax.vjp(gelu_fn, pre)
    grad_pre = pullback(grad_out.astype(jnp.float32))[0].astype(jnp.bfloat16)
    grad_agg = jnp.dot(weight_wide, grad_pre.astype(jnp.float32), precision=HIGH).astype(jnp.bfloat16)
    grad_agg_wide = grad_agg.astype(jnp.float32)
    hub_grads = jnp.dot(adjacency_wide, grad_agg_wide.T, precision=HIGH)
    hub_back = jnp.zeros((H, NODES), jnp.float32).at[:, hub_nodes].add(hub_grads.T)
    grad_blocks = grad_agg_wide.reshape(H, N_ROW, num_blocks, BLOCK)

    def back_step(total, reader):
        own_blocks = grad_blocks[:, reader]
        chosen = own_blocks[:, recv_targets[reader], :]
        sent_grads = jnp.einsum('fskj,skij->skfi', chosen, recv_tiles[reader].astype(jnp.float32), precision=HIGH)
        sent_grads = (sent_grads * live_of(reader)[:, :, None, None]).astype(jnp.bfloat16)
        place_from = (send_blocks[:, reader, :][:, :, None] == block_ids[None, None, :]).astype(jnp.float32)
        total = total + jnp.einsum('skfi,skb->fsbi', sent_grads.astype(jnp.float32), place_from, precision=HIGH)
        return (total, None)
    rem_back, _ = lax.scan(back_step, jnp.zeros((H, N_ROW, num_blocks, BLOCK), jnp.float32), jnp.arange(N_ROW).astype(jnp.int32))
    rem_back = rem_back.reshape(H, NODES)
    grad_in = (self_weight[None, :] * grad_agg_wide + hub_back + rem_back).astype(jnp.bfloat16)
    return (activation, grad_in)
```

```python
import functools

import jax
import jax.numpy as jnp
from jax import lax
from jax.experimental import pallas as pl
from jax.experimental.pallas import tpu as pltpu
from jax.sharding import PartitionSpec as P

BF = jnp.bfloat16
F32 = jnp.float32
VM = pl.BlockSpec(memory_space=pltpu.VMEM)
SM = pl.BlockSpec(memory_space=pltpu.SMEM)
MIB = 1 << 20
STEPS = (0, 1, 3, 2)
BACK = (0, 2, 1, 3)
NY, NZ, NC = 4, 4, 2
LIVE = 33


def row_perm(dy, dz, dc):
    pairs = []
    for y in range(NY):
        for z in range(NZ):
            for c in range(NC):
                to = (((y + dy) % NY) * NZ + (z + dz) % NZ) * NC + (c + dc) % NC
                pairs.append(((y * NZ + z) * NC + c, to))
    return pairs


def feat_perm(dh, dx):
    return [(h * 4 + x, ((h + dh) % 2) * 4 + (x + dx) % 4) for h in range(2) for x in range(4)]


def row_send(value, dy, dz, dc):
    return lax.ppermute(value, "row", row_perm(dy, dz, dc))


def feat_gather(value):
    across = lax.ppermute(value, "feat", feat_perm(1, 0))
    near = [lax.ppermute(value, "feat", feat_perm(0, k)) for k in STEPS[1:]]
    far = [lax.ppermute(across, "feat", feat_perm(0, k)) for k in STEPS[1:]]
    return [value, *near, across, *far]


def dot(a, b):
    return jnp.dot(a, b, preferred_element_type=F32)


def dot_nt(a, b):
    return lax.dot_general(a, b, (((1,), (1,)), ((), ())), preferred_element_type=F32)


def prep_kernel(me_ref, x_ref, ids_ref, sb_ref, out_ref):
    me = me_ref[0]
    window = lax.rem(me, 8)
    other = window + 1 - 2 * lax.rem(me, 2)
    for b in range(8):
        out_ref[b] = x_ref[:, b * 128 : (b + 1) * 128]
    rows = lax.broadcasted_iota(jnp.int32, (1024, 16), 0)
    pick = (rows == ids_ref[...]).astype(F32).astype(BF)
    hubs = dot(x_ref[...], pick).astype(BF)
    lane = lax.broadcasted_iota(jnp.int32, (16, 128), 1)
    which = lax.broadcasted_iota(jnp.int32, (16, 128), 0)
    place = (lane == window * 16 + which).astype(F32).astype(BF)
    extra = dot(hubs, place)
    lanes = lax.broadcasted_iota(jnp.int32, (32, 128), 1)
    ids = jnp.zeros((32, 128), F32)
    sb = sb_ref[...].astype(F32)
    for k in range(4):
        ids = ids + jnp.where(lanes == other * 16 + k, sb[:, k : k + 1], 0.0)
    out_ref[8, 0:32, :] = (extra[0:32] + ids).astype(BF)
    out_ref[8, 32:64, :] = extra[32:64].astype(BF)


def stack_kernel(p0, p1, p2, p3, out_ref):
    extra = jnp.zeros((64, 128), F32)
    for i, p in enumerate((p0, p1, p2, p3)):
        out_ref[i * 8 : (i + 1) * 8] = p[0:8]
        extra = extra + p[8].astype(F32)
    out_ref[32] = extra.astype(BF)


def place_of(me):
    return lax.div(me, 8), lax.rem(lax.div(me, 2), 4), lax.rem(me, 2)


def agg_kernel(
    me_ref, cnt_ref, tgt_ref, *rest
):
    srcs = rest[:8]
    tiles_ref, adj_ref, x_ref, self_ref, out_ref, sb_ref, acc, ids_v, ids_s, sem = rest[8:]
    me = me_ref[0]
    y, z, c = place_of(me)
    row = lax.broadcasted_iota(jnp.int32, (64, 128), 0)
    for a in range(8):
        here = jnp.where(row == me, srcs[a][32].astype(F32), 0.0)
        ids_v[a : a + 1, :] = jnp.sum(here, axis=0, keepdims=True).astype(jnp.int32)
    copy = pltpu.make_async_copy(ids_v, ids_s, sem)
    copy.start()
    acc[...] = jnp.zeros_like(acc)
    lane = lax.broadcasted_iota(jnp.int32, (64, 128), 1)
    parity = lax.rem(lax.div(lane, 16), 2)
    hub = jnp.zeros((64, 1024), F32)
    for j in range(4):
        sy = lax.rem(y - STEPS[j] + 4, 4)
        both = jnp.where(parity == c, srcs[j][32].astype(F32), srcs[4 + j][32].astype(F32)).astype(BF)
        hub = hub + dot(both, adj_ref[pl.ds(pl.multiple_of(sy * 128, 128), 128), :])
    copy.wait()
    for a in range(8):
        for i in range(8):
            sb_ref[a, i] = 0
    for a in range(8):
        j = a % 4
        cc = c if a < 4 else 1 - c
        sy = lax.rem(y - STEPS[j] + 4, 4)
        src = srcs[a]
        for i in range(4):
            sz = lax.rem(z - STEPS[i] + 4, 4)
            s = (sy * 4 + sz) * 2 + cc
            count = cnt_ref[s]
            parts = []
            for k in range(4):
                b = ids_s[a, (sz * 2 + 1 - cc) * 16 + k]
                sb_ref[s // 4, lax.rem(s, 4) * 4 + k] = b
                parts.append(dot(src[i * 8 + b], tiles_ref[s, k]))
            for k in range(4):
                t = jnp.where(k < count, tgt_ref[s, k], 8)
                acc[t] += parts[k]
    for b in range(8):
        cols = slice(b * 128, (b + 1) * 128)
        total = x_ref[:, cols].astype(F32) * self_ref[:, cols] + hub[:, cols] + acc[b]
        out_ref[:, cols] = total.astype(BF)


def mid_kernel(group_ref, *rest):
    aggs = rest[:8]
    ups = rest[8:16]
    wt_ref, w_ref, act_ref, ga_ref, full, pre, down = rest[16:]
    group = group_ref[0]
    h, x = lax.div(group, 4), lax.rem(group, 4)
    first = []
    for j in range(8):
        hh = h if j < 4 else 1 - h
        xx = lax.rem(x - STEPS[j % 4] + 4, 4)
        first.append(pl.multiple_of((hh * 4 + xx) * 64, 64))
    for j in range(8):
        full[pl.ds(first[j], 64), :] = aggs[j][...]
    own = w_ref[pl.ds(first[0], 64), :]
    for n in range(4):
        cols = slice(n * 256, (n + 1) * 256)
        pre[...] = dot(wt_ref[...], full[:, cols])
        for j in range(8):
            v = pre[pl.ds(first[j], 64), :]
            sq = v * v
            t = jnp.tanh(v * (0.7978845608 + (0.7978845608 * 0.044715) * sq))
            half = 0.5 + 0.5 * t
            if j == 0:
                act_ref[:, cols] = (v * half).astype(BF)
            slope = half + (0.5 * v) * (1.0 - t * t) * (
                0.7978845608 + (0.7978845608 * 3 * 0.044715) * sq
            )
            down[pl.ds(first[j], 64), :] = (ups[j][:, cols].astype(F32) * slope).astype(BF)
        grads = dot(own, down[...]).astype(BF)
        ga_ref[2 * n] = grads[:, :128]
        ga_ref[2 * n + 1] = grads[:, 128:]


def back_kernel(swap, me_ref, cnt_ref, tgt_ref, sb_ref, ga_ref, tiles_ref, adj_ref, o0, o1, o2, o3, acc):
    me = me_ref[0]
    y, z, c = place_of(me)
    cc = 1 - c if swap else c
    for j, out in enumerate((o0, o1, o2, o3)):
        sy = lax.rem(y + STEPS[j], 4)
        for i in range(4):
            sz = lax.rem(z + STEPS[i], 4)
            s = (sy * 4 + sz) * 2 + cc
            count = cnt_ref[s]
            acc[0:8] = jnp.zeros((8, 64, 128), F32)
            parts = [dot_nt(ga_ref[tgt_ref[s, k]], tiles_ref[s, k]) for k in range(4)]
            for k in range(4):
                b = jnp.where(k < count, sb_ref[s // 4, lax.rem(s, 4) * 4 + k], 8)
                acc[b] += parts[k]
            out[i * 8 : (i + 1) * 8] = acc[0:8].astype(BF)
        hubs = jnp.zeros((64, 128), F32)
        at = pl.ds(pl.multiple_of(sy * 128, 128), 128)
        for b in range(8):
            hubs = hubs + dot_nt(ga_ref[b], adj_ref[at, b * 128 : (b + 1) * 128])
        out[32] = hubs.astype(BF)


def sum_kernel(p0, p1, p2, p3, z0, z1, z2, z3):
    for i, out in enumerate((z0, z1, z2, z3)):
        for b in range(8):
            r = i * 8 + b
            out[b] = (p0[r].astype(F32) + p1[r].astype(F32) + p2[r].astype(F32) + p3[r].astype(F32)).astype(BF)
    extra = (p0[32].astype(F32) + p1[32].astype(F32) + p2[32].astype(F32) + p3[32].astype(F32)).astype(BF)
    for out in (z0, z1, z2, z3):
        out[8] = extra


def last_kernel(me_ref, z0, z1, z2, z3, ga_ref, self_ref, ids_ref, out_ref):
    window = lax.rem(me_ref[0], 8)

    def total(b):
        return z0[b].astype(F32) + z1[b].astype(F32) + z2[b].astype(F32) + z3[b].astype(F32)

    def halves(v):
        high = v.astype(BF)
        return high, (v - high.astype(F32)).astype(BF)

    lane = lax.broadcasted_iota(jnp.int32, (128, 16), 0)
    which = lax.broadcasted_iota(jnp.int32, (128, 16), 1)
    take = (lane == window * 16 + which).astype(F32).astype(BF)
    high, low = halves(total(8))
    high, low = halves(dot(high, take) + dot(low, take))
    node = lax.broadcasted_iota(jnp.int32, (16, 1024), 1)
    spread = (node == ids_ref[...]).astype(F32).astype(BF)
    hubs = dot(high, spread) + dot(low, spread)
    for b in range(8):
        cols = slice(b * 128, (b + 1) * 128)
        out_ref[:, cols] = (ga_ref[b].astype(F32) * self_ref[:, cols] + hubs[:, cols] + total(b)).astype(BF)


def call(kernel, name, outs, in_specs, args, scratch=(), limit=32, out_specs=None, flops=0, size=0):
    shapes = [jax.ShapeDtypeStruct(s, d) for s, d in outs]
    return pl.pallas_call(
        kernel,
        out_shape=shapes,
        in_specs=in_specs,
        out_specs=out_specs or [VM] * len(shapes),
        scratch_shapes=list(scratch),
        compiler_params=pltpu.CompilerParams(vmem_limit_bytes=limit * MIB),
        cost_estimate=pl.CostEstimate(flops=flops, bytes_accessed=size, transcendentals=0),
        name=name,
    )(*args)


def shards(
    node_feats,
    self_weight,
    hub_ids,
    hub_adjacency,
    send_blocks,
    recv_counts,
    recv_targets,
    recv_tiles,
    weight,
    grad_out,
):
    me = lax.axis_index("row").astype(jnp.int32).reshape(1)
    group = lax.axis_index("feat").astype(jnp.int32).reshape(1)
    counts = recv_counts.reshape(32)
    targets = recv_targets.reshape(32, 4)
    tiles = recv_tiles.reshape(32, 4, 128, 128)
    self_row = self_weight.reshape(1, 1024)
    part = ((9, 64, 128), BF)
    wide = ((LIVE, 64, 128), BF)

    (p0,) = call(
        prep_kernel, "prep", [part], [SM, VM, VM, VM],
        (me, node_feats, hub_ids.reshape(1, 16), send_blocks.reshape(32, 4)),
    )
    ps = [p0] + [row_send(p0, 0, k, 0) for k in STEPS[1:]]
    (a0,) = call(stack_kernel, "stack", [wide], [VM] * 4, ps)
    a0, grad_late = lax.optimization_barrier((a0, grad_out))
    own = [a0] + [row_send(a0, k, 0, 0) for k in STEPS[1:]]
    ups = feat_gather(grad_late)
    sibling = [row_send(a, 0, 0, 1) for a in own]
    agg, sb = call(
        agg_kernel, "aggregate",
        [((64, 1024), BF), ((8, 16), jnp.int32)],
        [SM] * 3 + [VM] * 12,
        (me, counts, targets, *own, *sibling, tiles, hub_adjacency, node_feats, self_row),
        scratch=[
            pltpu.VMEM((9, 64, 128), F32),
            pltpu.VMEM((8, 128), jnp.int32),
            pltpu.SMEM((8, 128), jnp.int32),
            pltpu.SemaphoreType.DMA,
        ],
        out_specs=[VM, SM],
    )
    aggs = feat_gather(agg)
    act, ga = call(
        mid_kernel, "middle",
        [((64, 1024), BF), ((8, 64, 128), BF)],
        [SM] + [VM] * 18,
        (group, *aggs, *ups, weight.T, weight),
        scratch=[
            pltpu.VMEM((512, 1024), BF),
            pltpu.VMEM((512, 256), F32),
            pltpu.VMEM((512, 256), BF),
        ],
    )
    back_args = (me, counts, targets, sb, ga, tiles, hub_adjacency)
    outs = []
    for swap in (True, False):
        outs.append(
            call(
                functools.partial(back_kernel, swap), "back_swap" if swap else "back_own",
                [wide] * 4, [SM] * 4 + [VM] * 3, back_args,
                scratch=[pltpu.VMEM((9, 64, 128), F32)],
            )
        )
    came = [row_send(v, 0, 0, 1) for v in outs[0]]
    both = [(a.astype(F32) + b.astype(F32)).astype(BF) for a, b in zip(outs[1], came)]
    ys = [both[0]] + [row_send(both[j], STEPS[j], 0, 0) for j in (1, 2, 3)]
    zs = call(sum_kernel, "sum_y", [part] * 4, [VM] * 4, ys)
    zs = [zs[0]] + [row_send(zs[i], 0, STEPS[i], 0) for i in (1, 2, 3)]
    (grad_in,) = call(
        last_kernel, "last", [((64, 1024), BF)], [SM] + [VM] * 7,
        (me, *zs, ga, self_row, hub_ids.reshape(16, 1)),
    )
    return (act, grad_in)


def solution(mesh):
    in_specs = (
        P("feat", "row"),
        P("row"),
        P("row"),
        P(None, "row"),
        P("row", None, None),
        P("row", None),
        P("row", None, None),
        P("row", None, None, None, None),
        P(),
        P("feat", "row"),
    )
    out_specs = (P("feat", "row"), P("feat", "row"))
    return jax.shard_map(shards, mesh=mesh, in_specs=in_specs, out_specs=out_specs, check_vma=False)
```

```python
import functools

import jax
import jax.numpy as jnp
from jax import lax
from jax.experimental import pallas as pl
from jax.experimental.pallas import tpu as pltpu
from jax.sharding import PartitionSpec as P

BF = jnp.bfloat16
F32 = jnp.float32
VM = pl.BlockSpec(memory_space=pltpu.VMEM)
HB = pl.BlockSpec(memory_space=pltpu.HBM)
ANY = pl.BlockSpec(memory_space=pl.ANY)
SM = pl.BlockSpec(memory_space=pltpu.SMEM)
MIB = 1 << 20
STEPS = (0, 1, 3, 2)
BACK = (0, 2, 1, 3)
NY, NZ, NC = 4, 4, 2
LIVE = 33
NA = 6
NB = 8 - NA
WIDE_A, WIDE_B = 4 * NA + 1, 4 * NB


def row_perm(dy, dz, dc):
    pairs = []
    for y in range(NY):
        for z in range(NZ):
            for c in range(NC):
                to = (((y + dy) % NY) * NZ + (z + dz) % NZ) * NC + (c + dc) % NC
                pairs.append(((y * NZ + z) * NC + c, to))
    return pairs


def feat_perm(dh, dx):
    return [(h * 4 + x, ((h + dh) % 2) * 4 + (x + dx) % 4) for h in range(2) for x in range(4)]


def row_send(value, dy, dz, dc):
    return lax.ppermute(value, "row", row_perm(dy, dz, dc))


def feat_gather(value):
    across = lax.ppermute(value, "feat", feat_perm(1, 0))
    near = [lax.ppermute(value, "feat", feat_perm(0, k)) for k in STEPS[1:]]
    far = [lax.ppermute(across, "feat", feat_perm(0, k)) for k in STEPS[1:]]
    return [value, *near, across, *far]


def dot(a, b):
    return jnp.dot(a, b, preferred_element_type=F32)


def dot_nt(a, b):
    return lax.dot_general(a, b, (((1,), (1,)), ((), ())), preferred_element_type=F32)


def dot_tn(a, b):
    return lax.dot_general(a, b, (((0,), (0,)), ((), ())), preferred_element_type=F32)


def here():
    me = lax.axis_index("row")
    return lax.div(me, 8), lax.rem(lax.div(me, 2), 4), lax.rem(me, 2)


def ahead(at, step):
    return lax.rem(at + step, 4)


def behind(at, step):
    return lax.rem(at + 4 - step, 4)


def prep_kernel(x_ref, ints_ref, out_ref):
    _, z, c = here()
    window = (z * 2 + c) * 16
    other = (z * 2 + 1 - c) * 16
    for b in range(8):
        out_ref[b] = x_ref[:, b * 128 : (b + 1) * 128]
    rows = lax.broadcasted_iota(jnp.int32, (1024, 16), 0)
    pick = (rows == ints_ref[9:10, 0:16]).astype(F32).astype(BF)
    hubs = dot(x_ref[...], pick).astype(BF)
    lane = lax.broadcasted_iota(jnp.int32, (16, 128), 1)
    which = lax.broadcasted_iota(jnp.int32, (16, 128), 0)
    extra = dot(hubs, (lane == window + which).astype(F32).astype(BF))
    lane = lax.broadcasted_iota(jnp.int32, (4, 128), 1)
    which = lax.broadcasted_iota(jnp.int32, (4, 128), 0)
    place = (lane == other + which).astype(F32)
    ids = dot_tn(ints_ref[0:4, :].astype(F32), place)
    out_ref[8, 0:32, :] = (extra[0:32] + ids).astype(BF)
    out_ref[8, 32:64, :] = extra[32:64].astype(BF)


def stack_kernel(p0, p1, p2, p3, out_ref):
    extra = jnp.zeros((64, 128), F32)
    for i, p in enumerate((p0, p1, p2, p3)):
        out_ref[i * 8 : (i + 1) * 8] = p[0:8]
        extra = extra + p[8].astype(F32)
    out_ref[32] = extra.astype(BF)


def pair_kernel(up_ref, far_ref, w_ref, tiles_ref, _, pair_ref, wt_ref, own_ref):
    pair_ref[0:64, :] = up_ref[...]
    pair_ref[64:128, :] = far_ref[...]
    wt_ref[...] = w_ref[...].T
    own_ref[...] = w_ref[pl.ds(pl.multiple_of(lax.axis_index("feat") * 64, 64), 64), :]


def slot_sums(swap, ints_ref, srcs, tiles_ref, sb_ref, acc, ids_v, ids_s, sem):
    y, z, c = here()
    me = (y * 4 + z) * 2 + c
    cc = 1 - c if swap else c
    row = lax.broadcasted_iota(jnp.int32, (64, 128), 0)
    ids_v[...] = jnp.zeros_like(ids_v)
    for j in range(4):
        mine = jnp.where(row == me, srcs[j][32].astype(F32), 0.0)
        ids_v[j : j + 1, :] = jnp.sum(mine, axis=0, keepdims=True).astype(jnp.int32)
    copy = pltpu.make_async_copy(ids_v, ids_s, sem)
    copy.start()
    copy.wait()
    for j in range(4):
        sy = behind(y, STEPS[j])
        for i in range(4):
            sz = behind(z, STEPS[i])
            s = (sy * 4 + sz) * 2 + cc
            count = ints_ref[8, s]
            parts = []
            for k in range(4):
                b = ids_s[j, (sz * 2 + 1 - cc) * 16 + k]
                sb_ref[sy, sz * 4 + k] = b
                parts.append(dot(srcs[j][i * 8 + b], tiles_ref[s, k]))
            for k in range(4):
                t = jnp.where(k < count, ints_ref[4 + k, s], 8)
                acc[t] += parts[k]


def agg_own_kernel(ints_ref, *rest):
    srcs = rest[:4]
    tiles_ref, out_ref, sb_ref, acc, *scratch = rest[4:]
    acc[...] = jnp.zeros_like(acc)
    slot_sums(False, ints_ref, srcs, tiles_ref, sb_ref, acc, *scratch)
    out_ref[...] = acc[0:8]


def agg_swap_kernel(ints_ref, *rest):
    srcs, owns = rest[:4], rest[4:8]
    tiles_ref, adj_ref, x_ref, self_ref, sum_ref, out_ref, sb_ref, acc, *scratch = rest[8:]
    y, _, c = here()
    acc[0:8] = sum_ref[...]
    acc[8] = jnp.zeros((64, 128), F32)
    slot_sums(True, ints_ref, srcs, tiles_ref, sb_ref, acc, *scratch)
    side = lax.rem(lax.div(lax.broadcasted_iota(jnp.int32, (64, 128), 1), 16), 2)
    hub = jnp.zeros((64, 1024), F32)
    for j in range(4):
        sy = behind(y, STEPS[j])
        both = jnp.where(side == c, owns[j][32].astype(F32), srcs[j][32].astype(F32)).astype(BF)
        hub = hub + dot(both, adj_ref[pl.ds(pl.multiple_of(sy * 128, 128), 128), :])
    for b in range(8):
        cols = slice(b * 128, (b + 1) * 128)
        total = x_ref[:, cols].astype(F32) * self_ref[:, cols] + hub[:, cols] + acc[b]
        out_ref[:, cols] = total.astype(BF)


def mid_kernel(*rest):
    aggs = rest[:8]
    ups = rest[8:12]
    wt_ref, own_ref, act_ref, ga_ref, full, pre, down = rest[12:]
    group = lax.axis_index("feat")
    h, x = lax.div(group, 4), lax.rem(group, 4)
    first = []
    for j in range(8):
        hh = h if j < 4 else 1 - h
        first.append(pl.multiple_of((hh * 4 + behind(x, STEPS[j % 4])) * 64, 64))
    for j in range(8):
        full[pl.ds(first[j], 64), :] = aggs[j][...]
    own = own_ref[...]
    for n in range(4):
        cols = slice(n * 256, (n + 1) * 256)
        pre[...] = dot(wt_ref[...], full[:, cols])
        for j in range(8):
            v = pre[pl.ds(first[j], 64), :]
            sq = v * v
            t = jnp.tanh(v * (0.7978845608 + (0.7978845608 * 0.044715) * sq))
            half = 0.5 + 0.5 * t
            if j == 0:
                act_ref[:, cols] = (v * half).astype(BF)
            slope = half + (0.5 * v) * (1.0 - t * t) * (
                0.7978845608 + (0.7978845608 * 3 * 0.044715) * sq
            )
            up = ups[j % 4][(j // 4) * 64 : (j // 4 + 1) * 64, cols]
            down[pl.ds(first[j], 64), :] = (up.astype(F32) * slope).astype(BF)
        grads = dot(own, down[...]).astype(BF)
        ga_ref[2 * n] = grads[:, :128]
        ga_ref[2 * n + 1] = grads[:, 128:]


def back_kernel(swap, ints_ref, sb_ref, ga_ref, tiles_ref, adj_ref, out, acc):
    y, z, c = here()
    cc = 1 - c if swap else c
    for j in range(4):
        sy = ahead(y, STEPS[j])
        hubs = jnp.zeros((64, 128), F32)
        at = pl.ds(pl.multiple_of(sy * 128, 128), 128)
        for b in range(8):
            hubs = hubs + dot_nt(ga_ref[b], adj_ref[at, b * 128 : (b + 1) * 128])
        out[128 + j] = hubs.astype(BF)
        for i in range(4):
            sz = ahead(z, STEPS[i])
            s = (sy * 4 + sz) * 2 + cc
            count = ints_ref[8, s]
            acc[0:8] = jnp.zeros((8, 64, 128), F32)
            parts = [dot_nt(ga_ref[ints_ref[4 + k, s]], tiles_ref[s, k]) for k in range(4)]
            for k in range(4):
                b = jnp.where(k < count, sb_ref[sy, sz * 4 + k], 8)
                acc[b] += parts[k]
            n = (j * 4 + i) * 8
            out[n : n + 8] = acc[0:8].astype(BF)


def add_kernel(a, b, *outs):
    def both(n):
        return (a[n].astype(F32) + b[n].astype(F32)).astype(BF)

    for j in range(4):
        for i in range(4):
            for r in range(8):
                total = both((j * 4 + i) * 8 + r)
                if r < NA:
                    outs[j][i * NA + r] = total
                else:
                    outs[4 + i][j * NB + r - NA] = total
        outs[j][4 * NA] = both(128 + j)


def four(refs, r):
    return (refs[0][r].astype(F32) + refs[1][r].astype(F32)) + (refs[2][r].astype(F32) + refs[3][r].astype(F32))


def sum_a_kernel(*refs):
    hubs = four(refs[:4], 4 * NA).astype(BF)
    for i in range(4):
        for b in range(NA):
            refs[4 + i][b] = four(refs[:4], i * NA + b).astype(BF)
        refs[4 + i][NA] = hubs


def sum_b_kernel(*refs):
    for j in range(4):
        for b in range(NB):
            refs[4 + j][b] = four(refs[:4], j * NB + b).astype(BF)


def last_kernel(*rest):
    pas, pbs = rest[:4], rest[4:8]
    ga_ref, self_ref, ids_ref, out_ref = rest[8:]
    _, z, c = here()

    def halves(v):
        high = v.astype(BF)
        return high, (v - high.astype(F32)).astype(BF)

    lane = lax.broadcasted_iota(jnp.int32, (128, 16), 0)
    which = lax.broadcasted_iota(jnp.int32, (128, 16), 1)
    take = (lane == (z * 2 + c) * 16 + which).astype(F32).astype(BF)
    high, low = halves(four(pas, NA))
    high, low = halves(dot(high, take) + dot(low, take))
    node = lax.broadcasted_iota(jnp.int32, (1024, 16), 0)
    spread = (node == ids_ref[...]).astype(F32).astype(BF)
    hubs = dot_nt(high, spread) + dot_nt(low, spread)
    for b in range(8):
        cols = slice(b * 128, (b + 1) * 128)
        total = four(pas, b) if b < NA else four(pbs, b - NA)
        out_ref[:, cols] = (ga_ref[b].astype(F32) * self_ref[:, cols] + hubs[:, cols] + total).astype(BF)


def call(kernel, name, outs, args, scalars=0, scratch=(), limit=8, out_specs=None, size=MIB, hbm=0, loose=0):
    shapes = [jax.ShapeDtypeStruct(s, d) for s, d in outs]
    return pl.pallas_call(
        kernel,
        out_shape=shapes,
        in_specs=[HB] * hbm + [SM] * scalars + [VM] * (len(args) - scalars - hbm - loose) + [ANY] * loose,
        out_specs=out_specs or [VM] * len(shapes),
        scratch_shapes=list(scratch),
        compiler_params=pltpu.CompilerParams(vmem_limit_bytes=limit * MIB),
        cost_estimate=pl.CostEstimate(flops=0, bytes_accessed=size, transcendentals=0),
        name=name,
    )(*args)


def shards(
    node_feats,
    self_weight,
    hub_ids,
    hub_adjacency,
    send_blocks,
    recv_counts,
    recv_targets,
    recv_tiles,
    weight,
    grad_out,
):
    ids = hub_ids.reshape(1, 16)
    ints = jnp.concatenate(
        [
            jnp.transpose(send_blocks, (0, 2, 1)).reshape(4, 32),
            jnp.transpose(recv_targets, (0, 2, 1)).reshape(4, 32),
            recv_counts,
            jnp.concatenate([ids, ids], axis=1),
        ],
        axis=0,
    )
    tiles = recv_tiles.reshape(32, 4, 128, 128)
    self_row = self_weight.reshape(1, 1024)

    def shape(n):
        return ((n, 64, 128), BF)

    (p0,) = call(prep_kernel, "prep", [shape(9)], (node_feats, ints))
    ps = [p0] + [row_send(p0, 0, k, 0) for k in STEPS[1:]]
    (s0,) = call(stack_kernel, "stack", [shape(LIVE)], ps)
    owns = [s0] + [row_send(s0, k, 0, 0) for k in STEPS[1:]]
    up, _ = lax.optimization_barrier((grad_out, p0))
    up_far = lax.ppermute(up, "feat", feat_perm(1, 0))
    pair, wt, own = call(
        pair_kernel, "pair", [((128, 1024), BF), ((512, 512), BF), ((64, 512), BF)],
        (grad_out, up_far, weight, tiles, s0), 0, (), 12, loose=1,
    )
    ups = [pair] + [lax.ppermute(pair, "feat", feat_perm(0, k)) for k in STEPS[1:]]
    late = lax.optimization_barrier((owns[3], *ups))
    owns[3], ups = late[0], late[1:]
    swaps = [row_send(v, 0, 0, 1) for v in owns]
    slots = [
        pltpu.VMEM((9, 64, 128), F32),
        pltpu.VMEM((8, 128), jnp.int32),
        pltpu.SMEM((8, 128), jnp.int32),
        pltpu.SemaphoreType.DMA,
    ]
    listed = ((4, 16), jnp.int32)
    part, sb_own = call(
        agg_own_kernel, "agg_own", [((8, 64, 128), F32), listed],
        (ints, *owns, tiles), 1, slots, 16, [VM, SM], 8 * MIB,
    )
    agg, sb_swap = call(
        agg_swap_kernel, "agg_swap", [((64, 1024), BF), listed],
        (ints, *swaps, *owns, tiles, hub_adjacency, node_feats, self_row, part),
        1, slots, 16, [VM, SM], 8 * MIB,
    )
    aggs = feat_gather(agg)
    act, ga = call(
        mid_kernel, "middle", [((64, 1024), BF), shape(8)], (*aggs, *ups, wt, own), 0,
        [
            pltpu.VMEM((512, 1024), BF),
            pltpu.VMEM((512, 256), F32),
            pltpu.VMEM((512, 256), BF),
        ],
        16, None, 16 * MIB,
    )
    outs = []
    for swap in (True, False):
        (out,) = call(
            functools.partial(back_kernel, swap), "back_swap" if swap else "back_own",
            [shape(132)], (ints, sb_swap if swap else sb_own, ga, tiles, hub_adjacency), 2,
            [pltpu.VMEM((9, 64, 128), F32)], 16, None, 8 * MIB,
        )
        outs.append(out)
    came = row_send(outs[0], 0, 0, 1)
    both = call(add_kernel, "add", [shape(WIDE_A)] * 4 + [shape(WIDE_B)] * 4, (outs[1], came), 0, (), 16)
    ras = [both[0]] + [row_send(both[j], STEPS[j], 0, 0) for j in (1, 2, 3)]
    rbs = [both[4]] + [row_send(both[4 + i], 0, STEPS[i], 0) for i in (1, 2, 3)]
    zas = call(sum_a_kernel, "sum_a", [shape(NA + 1)] * 4, ras)
    ybs = call(sum_b_kernel, "sum_b", [shape(NB)] * 4, rbs)
    zas = [zas[0]] + [row_send(zas[i], 0, STEPS[i], 0) for i in (1, 2, 3)]
    ybs = [ybs[0]] + [row_send(ybs[j], STEPS[j], 0, 0) for j in (1, 2, 3)]
    (grad_in,) = call(last_kernel, "last", [((64, 1024), BF)], (*zas, *ybs, ga, self_row, ids))
    return (act, grad_in)


def solution(mesh):
    in_specs = (
        P("feat", "row"),
        P("row"),
        P("row"),
        P(None, "row"),
        P("row", None, None),
        P("row", None),
        P("row", None, None),
        P("row", None, None, None, None),
        P(),
        P("feat", "row"),
    )
    out_specs = (P("feat", "row"), P("feat", "row"))
    return jax.shard_map(shards, mesh=mesh, in_specs=in_specs, out_specs=out_specs, check_vma=False)
```

```python
import functools

import jax
import jax.numpy as jnp
from jax import lax
from jax.experimental import pallas as pl
from jax.experimental.pallas import tpu as pltpu
from jax.sharding import PartitionSpec as P

BF = jnp.bfloat16
F32 = jnp.float32
VM = pl.BlockSpec(memory_space=pltpu.VMEM)
HB = pl.BlockSpec(memory_space=pltpu.HBM)
ANY = pl.BlockSpec(memory_space=pl.ANY)
SM = pl.BlockSpec(memory_space=pltpu.SMEM)
MIB = 1 << 20
STEPS = (0, 1, 3, 2)
BACK = (0, 2, 1, 3)
NY, NZ, NC = 4, 4, 2
EARLY = False
LIVE = 33
NA = 6
NB = 8 - NA
WIDE_A, WIDE_B = 4 * NA + 1, 4 * NB


def row_perm(dy, dz, dc):
    pairs = []
    for y in range(NY):
        for z in range(NZ):
            for c in range(NC):
                to = (((y + dy) % NY) * NZ + (z + dz) % NZ) * NC + (c + dc) % NC
                pairs.append(((y * NZ + z) * NC + c, to))
    return pairs


def feat_perm(dh, dx):
    return [(h * 4 + x, ((h + dh) % 2) * 4 + (x + dx) % 4) for h in range(2) for x in range(4)]


def row_send(value, dy, dz, dc):
    return lax.ppermute(value, "row", row_perm(dy, dz, dc))


def feat_gather(value):
    across = lax.ppermute(value, "feat", feat_perm(1, 0))
    near = [lax.ppermute(value, "feat", feat_perm(0, k)) for k in STEPS[1:]]
    far = [lax.ppermute(across, "feat", feat_perm(0, k)) for k in STEPS[1:]]
    return [value, *near, across, *far]


def dot(a, b):
    return jnp.dot(a, b, preferred_element_type=F32)


def dot_nt(a, b):
    return lax.dot_general(a, b, (((1,), (1,)), ((), ())), preferred_element_type=F32)


def dot_tn(a, b):
    return lax.dot_general(a, b, (((0,), (0,)), ((), ())), preferred_element_type=F32)


def here():
    me = lax.axis_index("row")
    return lax.div(me, 8), lax.rem(lax.div(me, 2), 4), lax.rem(me, 2)


def ahead(at, step):
    return lax.rem(at + step, 4)


def behind(at, step):
    return lax.rem(at + 4 - step, 4)


def prep_kernel(x_ref, ints_ref, out_ref):
    _, z, c = here()
    window = (z * 2 + c) * 16
    other = (z * 2 + 1 - c) * 16
    for b in range(8):
        out_ref[b] = x_ref[:, b * 128 : (b + 1) * 128]
    rows = lax.broadcasted_iota(jnp.int32, (1024, 16), 0)
    pick = (rows == ints_ref[9:10, 0:16]).astype(F32).astype(BF)
    hubs = dot(x_ref[...], pick).astype(BF)
    lane = lax.broadcasted_iota(jnp.int32, (16, 128), 1)
    which = lax.broadcasted_iota(jnp.int32, (16, 128), 0)
    extra = dot(hubs, (lane == window + which).astype(F32).astype(BF))
    lane = lax.broadcasted_iota(jnp.int32, (4, 128), 1)
    which = lax.broadcasted_iota(jnp.int32, (4, 128), 0)
    place = (lane == other + which).astype(F32)
    ids = dot_tn(ints_ref[0:4, :].astype(F32), place)
    out_ref[8, 0:32, :] = (extra[0:32] + ids).astype(BF)
    out_ref[8, 32:64, :] = extra[32:64].astype(BF)


def stack_kernel(p0, p1, p2, p3, out_ref):
    extra = jnp.zeros((64, 128), F32)
    for i, p in enumerate((p0, p1, p2, p3)):
        out_ref[i * 8 : (i + 1) * 8] = p[0:8]
        extra = extra + p[8].astype(F32)
    out_ref[32] = extra.astype(BF)


def group_rows():
    group = lax.axis_index("feat")
    h, x = lax.div(group, 4), lax.rem(group, 4)
    first = []
    for j in range(8):
        hh = h if j < 4 else 1 - h
        first.append(pl.multiple_of((hh * 4 + behind(x, STEPS[j % 4])) * 64, 64))
    return first


def pair_kernel(up_ref, far_ref, w_ref, tiles_ref, _, pair_ref, wt_ref, own_ref, held):
    pair_ref[0:64, :] = up_ref[...]
    pair_ref[64:128, :] = far_ref[...]
    first = group_rows()
    for j in range(8):
        held[j * 64 : (j + 1) * 64, :] = w_ref[pl.ds(first[j], 64), :]
    held[...] = held[...].T
    for j in range(8):
        wt_ref[j * 64 : (j + 1) * 64, :] = held[pl.ds(first[j], 64), :]
    own_ref[...] = wt_ref[:, 0:128].T


def agg_kernel(part, ints_ref, *rest):
    owns, swaps = rest[:2], rest[2:4]
    if part == 0:
        tiles_ref, adj_ref, x_ref, self_ref, out_ref, sb_ref, acc, ids_v, ids_s, sem = rest[4:]
    else:
        tiles_ref, adj_ref, sum_ref, out_ref, sb_ref, acc, ids_v, ids_s, sem = rest[4:]
    y, z, c = here()
    me = (y * 4 + z) * 2 + c
    row = lax.broadcasted_iota(jnp.int32, (64, 128), 0)
    ids_v[...] = jnp.zeros_like(ids_v)
    for n, src in enumerate((*owns, *swaps)):
        mine = jnp.where(row == me, src[32].astype(F32), 0.0)
        ids_v[n : n + 1, :] = jnp.sum(mine, axis=0, keepdims=True).astype(jnp.int32)
    copy = pltpu.make_async_copy(ids_v, ids_s, sem)
    copy.start()
    side = lax.rem(lax.div(lax.broadcasted_iota(jnp.int32, (64, 128), 1), 16), 2)
    hub = jnp.zeros((64, 1024), F32)
    for n in range(2):
        sy = behind(y, STEPS[part * 2 + n])
        both = jnp.where(side == c, owns[n][32].astype(F32), swaps[n][32].astype(F32)).astype(BF)
        hub = hub + dot(both, adj_ref[pl.ds(pl.multiple_of(sy * 128, 128), 128), :])
    for b in range(8):
        cols = slice(b * 128, (b + 1) * 128)
        if part == 0:
            acc[b] = x_ref[:, cols].astype(F32) * self_ref[:, cols] + hub[:, cols]
        else:
            acc[b] = sum_ref[b] + hub[:, cols]
    acc[8] = jnp.zeros((64, 128), F32)
    copy.wait()
    for m, srcs in enumerate((owns, swaps)):
        cc = 1 - c if m else c
        for n in range(2):
            sy = behind(y, STEPS[part * 2 + n])
            for i in range(4):
                sz = behind(z, STEPS[i])
                s = (sy * 4 + sz) * 2 + cc
                count = ints_ref[8, s]
                parts = []
                for k in range(4):
                    b = ids_s[m * 2 + n, (sz * 2 + 1 - cc) * 16 + k]
                    sb_ref[m * 2 + n, sz * 4 + k] = b
                    parts.append(dot(srcs[n][i * 8 + b], tiles_ref[s, k]))
                for k in range(4):
                    t = jnp.where(k < count, ints_ref[4 + k, s], 8)
                    acc[t] += parts[k]
    if part == 0:
        out_ref[...] = acc[0:8]
    else:
        for b in range(8):
            out_ref[:, b * 128 : (b + 1) * 128] = acc[b].astype(BF)


def mid_kernel(*rest):
    aggs, ups = rest[:8], rest[8:12]
    wt_ref, own_ref, adj_ref, act_ref, ga_ref, hub_ref, full, pre, down = rest[12:]
    hubs = jnp.zeros((64, 512), F32)
    for j in range(8):
        full[j * 64 : (j + 1) * 64, :] = aggs[j][...]
    for n in range(4):
        cols = slice(n * 256, (n + 1) * 256)
        pre[n % 2] = dot(wt_ref[...], full[:, cols])
        for j in range(8):
            rows = slice(j * 64, (j + 1) * 64)
            v = pre[n % 2, rows]
            sq = v * v
            t = jnp.tanh(v * (0.7978845608 + (0.7978845608 * 0.044715) * sq))
            half = 0.5 + 0.5 * t
            if j == 0:
                act_ref[:, cols] = (v * half).astype(BF)
            slope = half + (0.5 * v) * (1.0 - t * t) * (
                0.7978845608 + (0.7978845608 * 3 * 0.044715) * sq
            )
            up = ups[j % 4][(j // 4) * 64 : (j // 4 + 1) * 64, cols]
            down[n % 2, rows] = (up.astype(F32) * slope).astype(BF)
        grads = dot(own_ref[0:64, :], down[n % 2]).astype(BF)
        ga_ref[2 * n] = grads[:, :128]
        ga_ref[2 * n + 1] = grads[:, 128:]
        hubs = hubs + dot_nt(grads, adj_ref[:, cols])
    for j in range(4):
        hub_ref[j] = hubs[:, j * 128 : (j + 1) * 128]


GROUPS = ((1, 3), (0, 2))


def back_kernel(swap, part, ints_ref, sb0_ref, sb1_ref, ga_ref, tiles_ref, hub_ref, *rest):
    out, acc = rest[-2:]
    y, z, c = here()
    cc = 1 - c if swap else c
    none = jnp.zeros((64, 128), BF)
    for g, j in enumerate(GROUPS[part]):
        sy = ahead(y, STEPS[j])
        sb_ref = (sb0_ref, sb1_ref)[BACK[j] // 2]
        sb_row = (2 if swap else 0) + BACK[j] % 2
        out[64 + g] = hub_ref[sy].astype(BF)
        for i in range(4):
            sz = ahead(z, STEPS[i])
            s = (sy * 4 + sz) * 2 + cc
            count = ints_ref[8, s]
            acc[0:8] = jnp.zeros((8, 64, 128), F32)
            parts = []
            for k in (0, 2):
                one, two = (ga_ref[ints_ref[4 + k + n, s]] for n in range(2))
                rows = [jnp.concatenate([one, none], axis=1), jnp.concatenate([none, two], axis=1)]
                pair = jnp.concatenate([tiles_ref[s, k], tiles_ref[s, k + 1]], axis=1)
                sums = dot_nt(jnp.concatenate(rows, axis=0), pair)
                parts += [sums[:64], sums[64:]]
            for k in range(4):
                b = jnp.where(k < count, sb_ref[sb_row, sz * 4 + k], 8)
                acc[b] += parts[k]
            n = (g * 4 + i) * 8
            out[n : n + 8] = acc[0:8].astype(BF)


def both(a, b, n):
    return (a[n].astype(F32) + b[n].astype(F32)).astype(BF)


def add_first_kernel(a, b, *outs):
    for g in range(2):
        for i in range(4):
            for r in range(NA):
                outs[g][i * NA + r] = both(a, b, (g * 4 + i) * 8 + r)
        outs[g][4 * NA] = both(a, b, 64 + g)


def add_second_kernel(a0, b0, a, b, *outs):
    add_first_kernel(a, b, *outs[:2])
    for part, (p, q) in enumerate(((a0, b0), (a, b))):
        for g, j in enumerate(GROUPS[part]):
            for i in range(4):
                for r in range(NB):
                    outs[2 + i][j * NB + r] = both(p, q, (g * 4 + i) * 8 + NA + r)


def four(refs, r):
    return (refs[0][r].astype(F32) + refs[1][r].astype(F32)) + (refs[2][r].astype(F32) + refs[3][r].astype(F32))


def sum_a_kernel(*refs):
    hubs = four(refs[:4], 4 * NA).astype(BF)
    for i in range(4):
        for b in range(NA):
            refs[4 + i][b] = four(refs[:4], i * NA + b).astype(BF)
        refs[4 + i][NA] = hubs


def sum_b_kernel(*refs):
    for j in range(4):
        for b in range(NB):
            refs[4 + j][b] = four(refs[:4], j * NB + b).astype(BF)


def last_kernel(*rest):
    pas, pbs = rest[:4], rest[4:8]
    ga_ref, self_ref, ids_ref, out_ref = rest[8:]
    _, z, c = here()

    def halves(v):
        high = v.astype(BF)
        return high, (v - high.astype(F32)).astype(BF)

    lane = lax.broadcasted_iota(jnp.int32, (128, 16), 0)
    which = lax.broadcasted_iota(jnp.int32, (128, 16), 1)
    take = (lane == (z * 2 + c) * 16 + which).astype(F32).astype(BF)
    high, low = halves(four(pas, NA))
    high, low = halves(dot(high, take) + dot(low, take))
    node = lax.broadcasted_iota(jnp.int32, (1024, 16), 0)
    spread = (node == ids_ref[...]).astype(F32).astype(BF)
    hubs = dot_nt(high, spread) + dot_nt(low, spread)
    for b in range(8):
        cols = slice(b * 128, (b + 1) * 128)
        total = four(pas, b) if b < NA else four(pbs, b - NA)
        out_ref[:, cols] = (ga_ref[b].astype(F32) * self_ref[:, cols] + hubs[:, cols] + total).astype(BF)


def call(kernel, name, outs, args, scalars=0, scratch=(), limit=8, out_specs=None, size=MIB, hbm=0, loose=0):
    shapes = [jax.ShapeDtypeStruct(s, d) for s, d in outs]
    return pl.pallas_call(
        kernel,
        out_shape=shapes,
        in_specs=[HB] * hbm + [SM] * scalars + [VM] * (len(args) - scalars - hbm - loose) + [ANY] * loose,
        out_specs=out_specs or [VM] * len(shapes),
        scratch_shapes=list(scratch),
        compiler_params=pltpu.CompilerParams(vmem_limit_bytes=limit * MIB),
        cost_estimate=pl.CostEstimate(flops=0, bytes_accessed=size, transcendentals=0),
        name=name,
    )(*args)


def shards(
    node_feats,
    self_weight,
    hub_ids,
    hub_adjacency,
    send_blocks,
    recv_counts,
    recv_targets,
    recv_tiles,
    weight,
    grad_out,
):
    ids = hub_ids.reshape(1, 16)
    ints = jnp.concatenate(
        [
            jnp.transpose(send_blocks, (0, 2, 1)).reshape(4, 32),
            jnp.transpose(recv_targets, (0, 2, 1)).reshape(4, 32),
            recv_counts,
            jnp.concatenate([ids, ids], axis=1),
        ],
        axis=0,
    )
    tiles = recv_tiles.reshape(32, 4, 128, 128)
    self_row = self_weight.reshape(1, 1024)

    def shape(n):
        return ((n, 64, 128), BF)

    (p0,) = call(prep_kernel, "prep", [shape(9)], (node_feats, ints))
    ps = [p0] + [row_send(p0, 0, k, 0) for k in STEPS[1:]]
    (s0,) = call(stack_kernel, "stack", [shape(LIVE)], ps)
    owns = [s0] + [row_send(s0, k, 0, 0) for k in STEPS[1:]]
    up, _ = lax.optimization_barrier((grad_out, s0))
    up_far = lax.ppermute(up, "feat", feat_perm(1, 0))
    pair, wt, own = call(
        pair_kernel, "pair", [((128, 1024), BF), ((512, 512), BF), ((128, 512), BF)],
        (grad_out, up_far, weight, tiles, s0), 0, [pltpu.VMEM((512, 512), BF)], 12, loose=1,
    )
    slots = [
        pltpu.VMEM((9, 64, 128), F32),
        pltpu.VMEM((8, 128), jnp.int32),
        pltpu.SMEM((8, 128), jnp.int32),
        pltpu.SemaphoreType.DMA,
    ]
    listed = ((4, 16), jnp.int32)
    swaps = [row_send(v, 0, 0, 1) for v in owns[:2]]
    part, sb0 = call(
        functools.partial(agg_kernel, 0), "agg_first", [((8, 64, 128), F32), listed],
        (ints, *owns[:2], *swaps, tiles, hub_adjacency, node_feats, self_row), 1, slots, 16, [VM, SM], 8 * MIB,
    )
    later, _ = lax.optimization_barrier((pair, part)) if EARLY else (pair, part)
    ups = [pair] + [lax.ppermute(v, "feat", feat_perm(0, k)) for v, k in zip((pair, pair, later), (2, 1, 3))]
    ups = [ups[0], ups[2], ups[3], ups[1]]
    late = lax.optimization_barrier((owns[3], *ups))
    owns[3], ups = late[0], late[1:]
    swaps = [row_send(v, 0, 0, 1) for v in owns[2:]]
    agg, sb1 = call(
        functools.partial(agg_kernel, 1), "agg_second", [((64, 1024), BF), listed],
        (ints, *owns[2:], *swaps, tiles, hub_adjacency, part), 1, slots, 16, [VM, SM], 8 * MIB,
    )
    aggs = feat_gather(agg)
    act, ga, hubs = call(
        mid_kernel, "middle", [((64, 1024), BF), shape(8), ((4, 64, 128), F32)], (*aggs, *ups, wt, own, hub_adjacency), 0,
        [
            pltpu.VMEM((512, 1024), BF),
            pltpu.VMEM((2, 512, 256), F32),
            pltpu.VMEM((2, 512, 256), BF),
        ],
        16, None, 16 * MIB,
    )

    def back(swap, part, *tokens):
        (out,) = call(
            functools.partial(back_kernel, swap, part), "back_swap" if swap else "back_own", [shape(66)],
            (ints, sb0, sb1, ga, tiles, hubs, *tokens), 3, [slots[0]], 16, None, 4 * MIB,
            loose=len(tokens),
        )
        return out

    swap0 = back(True, 0)
    came0 = row_send(swap0, 0, 0, 1)
    swap1 = back(True, 1, swap0)
    came1 = row_send(swap1, 0, 0, 1)
    own0 = back(False, 0, swap1)
    sums = [None] * 4
    sums[1], sums[3] = call(add_first_kernel, "add_first", [shape(WIDE_A)] * 2, (own0, came0))
    own1 = back(False, 1, sums[3])
    sums[0], sums[2], *bs = call(
        add_second_kernel, "add_second", [shape(WIDE_A)] * 2 + [shape(WIDE_B)] * 4, (own0, came0, own1, came1), 0, (), 12
    )
    both = [*sums, *bs]
    ras = [both[0]] + [row_send(both[j], STEPS[j], 0, 0) for j in (1, 2, 3)]
    rbs = [both[4]] + [row_send(both[4 + i], 0, STEPS[i], 0) for i in (1, 2, 3)]
    zas = call(sum_a_kernel, "sum_a", [shape(NA + 1)] * 4, ras)
    ybs = call(sum_b_kernel, "sum_b", [shape(NB)] * 4, rbs)
    zas = [zas[0]] + [row_send(zas[i], 0, STEPS[i], 0) for i in (1, 2, 3)]
    ybs = [ybs[0]] + [row_send(ybs[j], STEPS[j], 0, 0) for j in (1, 2, 3)]
    (grad_in,) = call(last_kernel, "last", [((64, 1024), BF)], (*zas, *ybs, ga, self_row, ids))
    return (act, grad_in)


def solution(mesh):
    in_specs = (
        P("feat", "row"),
        P("row"),
        P("row"),
        P(None, "row"),
        P("row", None, None),
        P("row", None),
        P("row", None, None),
        P("row", None, None, None, None),
        P(),
        P("feat", "row"),
    )
    out_specs = (P("feat", "row"), P("feat", "row"))
    return jax.shard_map(shards, mesh=mesh, in_specs=in_specs, out_specs=out_specs, check_vma=False)
```

```python
import functools

import jax
import jax.numpy as jnp
from jax import lax
from jax.experimental import pallas as pl
from jax.experimental.pallas import tpu as pltpu
from jax.sharding import PartitionSpec as P

BF = jnp.bfloat16
F32 = jnp.float32
VM = pl.BlockSpec(memory_space=pltpu.VMEM)
HB = pl.BlockSpec(memory_space=pltpu.HBM)
ANY = pl.BlockSpec(memory_space=pl.ANY)
SM = pl.BlockSpec(memory_space=pltpu.SMEM)
MIB = 1 << 20
STEPS = (0, 1, 3, 2)
BACK = (0, 2, 1, 3)
NY, NZ, NC = 4, 4, 2
EARLY = False
LIVE = 33


def row_perm(dy, dz, dc):
    pairs = []
    for y in range(NY):
        for z in range(NZ):
            for c in range(NC):
                to = (((y + dy) % NY) * NZ + (z + dz) % NZ) * NC + (c + dc) % NC
                pairs.append(((y * NZ + z) * NC + c, to))
    return pairs


def feat_perm(dh, dx):
    return [(h * 4 + x, ((h + dh) % 2) * 4 + (x + dx) % 4) for h in range(2) for x in range(4)]


def row_send(value, dy, dz, dc):
    return lax.ppermute(value, "row", row_perm(dy, dz, dc))


def feat_gather(value):
    across = lax.ppermute(value, "feat", feat_perm(1, 0))
    near = [lax.ppermute(value, "feat", feat_perm(0, k)) for k in STEPS[1:]]
    far = [lax.ppermute(across, "feat", feat_perm(0, k)) for k in STEPS[1:]]
    return [value, *near, across, *far]


def dot(a, b):
    return jnp.dot(a, b, preferred_element_type=F32)


def dot_nt(a, b):
    return lax.dot_general(a, b, (((1,), (1,)), ((), ())), preferred_element_type=F32)


def dot_tn(a, b):
    return lax.dot_general(a, b, (((0,), (0,)), ((), ())), preferred_element_type=F32)


def here():
    me = lax.axis_index("row")
    return lax.div(me, 8), lax.rem(lax.div(me, 2), 4), lax.rem(me, 2)


def ahead(at, step):
    return lax.rem(at + step, 4)


def behind(at, step):
    return lax.rem(at + 4 - step, 4)


def prep_kernel(x_ref, ints_ref, out_ref):
    _, z, c = here()
    window = (z * 2 + c) * 16
    other = (z * 2 + 1 - c) * 16
    for b in range(8):
        out_ref[b] = x_ref[:, b * 128 : (b + 1) * 128]
    rows = lax.broadcasted_iota(jnp.int32, (1024, 16), 0)
    pick = (rows == ints_ref[9:10, 0:16]).astype(F32).astype(BF)
    hubs = dot(x_ref[...], pick).astype(BF)
    lane = lax.broadcasted_iota(jnp.int32, (16, 128), 1)
    which = lax.broadcasted_iota(jnp.int32, (16, 128), 0)
    extra = dot(hubs, (lane == window + which).astype(F32).astype(BF))
    lane = lax.broadcasted_iota(jnp.int32, (4, 128), 1)
    which = lax.broadcasted_iota(jnp.int32, (4, 128), 0)
    place = (lane == other + which).astype(F32)
    ids = dot_tn(ints_ref[0:4, :].astype(F32), place)
    out_ref[8, 0:32, :] = (extra[0:32] + ids).astype(BF)
    out_ref[8, 32:64, :] = extra[32:64].astype(BF)


def stack_kernel(p0, p1, p2, p3, *rest):
    out_ref = rest[-1]
    extra = jnp.zeros((64, 128), F32)
    for i, p in enumerate((p0, p1, p2, p3)):
        out_ref[i * 8 : (i + 1) * 8] = p[0:8]
        extra = extra + p[8].astype(F32)
    out_ref[32] = extra.astype(BF)


def group_rows():
    group = lax.axis_index("feat")
    h, x = lax.div(group, 4), lax.rem(group, 4)
    first = []
    for j in range(8):
        hh = h if j < 4 else 1 - h
        first.append(pl.multiple_of((hh * 4 + behind(x, STEPS[j % 4])) * 64, 64))
    return first


def weight_kernel(w_ref, tiles_ref, _, wt_ref, own_ref, held):
    first = group_rows()
    for j in range(8):
        held[j * 64 : (j + 1) * 64, :] = w_ref[pl.ds(first[j], 64), :]
    held[...] = held[...].T
    for j in range(8):
        wt_ref[j * 64 : (j + 1) * 64, :] = held[pl.ds(first[j], 64), :]
    own_ref[...] = wt_ref[:, 0:128].T


def agg_kernel(part, ints_ref, *rest):
    owns, swaps = rest[:2], rest[2:4]
    if part == 0:
        tiles_ref, adj_ref, x_ref, self_ref, out_ref, sb_ref, acc, ids_v, ids_s, sem = rest[4:]
    else:
        tiles_ref, adj_ref, sum_ref, out_ref, sb_ref, acc, ids_v, ids_s, sem = rest[4:]
    y, z, c = here()
    me = (y * 4 + z) * 2 + c
    row = lax.broadcasted_iota(jnp.int32, (64, 128), 0)
    ids_v[...] = jnp.zeros_like(ids_v)
    for n, src in enumerate((*owns, *swaps)):
        mine = jnp.where(row == me, src[32].astype(F32), 0.0)
        ids_v[n : n + 1, :] = jnp.sum(mine, axis=0, keepdims=True).astype(jnp.int32)
    copy = pltpu.make_async_copy(ids_v, ids_s, sem)
    copy.start()
    side = lax.rem(lax.div(lax.broadcasted_iota(jnp.int32, (64, 128), 1), 16), 2)
    hub = jnp.zeros((64, 1024), F32)
    for n in range(2):
        sy = behind(y, STEPS[part * 2 + n])
        both = jnp.where(side == c, owns[n][32].astype(F32), swaps[n][32].astype(F32)).astype(BF)
        hub = hub + dot(both, adj_ref[pl.ds(pl.multiple_of(sy * 128, 128), 128), :])
    for b in range(8):
        cols = slice(b * 128, (b + 1) * 128)
        if part == 0:
            acc[b] = x_ref[:, cols].astype(F32) * self_ref[:, cols] + hub[:, cols]
        else:
            acc[b] = sum_ref[b] + hub[:, cols]
    acc[8] = jnp.zeros((64, 128), F32)
    copy.wait()
    for m, srcs in enumerate((owns, swaps)):
        cc = 1 - c if m else c
        for n in range(2):
            sy = behind(y, STEPS[part * 2 + n])
            for i in range(4):
                sz = behind(z, STEPS[i])
                s = (sy * 4 + sz) * 2 + cc
                count = ints_ref[8, s]
                parts = []
                for k in range(4):
                    b = ids_s[m * 2 + n, (sz * 2 + 1 - cc) * 16 + k]
                    sb_ref[m * 2 + n, sz * 4 + k] = b
                    parts.append(dot(srcs[n][i * 8 + b], tiles_ref[s, k]))
                for k in range(4):
                    t = jnp.where(k < count, ints_ref[4 + k, s], 8)
                    acc[t] += parts[k]
    if part == 0:
        out_ref[...] = acc[0:8]
    else:
        for b in range(8):
            out_ref[:, b * 128 : (b + 1) * 128] = acc[b].astype(BF)


def mid_kernel(*rest):
    aggs, ups = rest[:8], rest[8:16]
    wt_ref, own_ref, adj_ref, act_ref, ga_ref, hub_ref, full, pre, down = rest[16:]
    hubs = jnp.zeros((64, 512), F32)
    for j in range(8):
        full[j * 64 : (j + 1) * 64, :] = aggs[j][...]
    for n in range(4):
        cols = slice(n * 256, (n + 1) * 256)
        pre[n % 2] = dot(wt_ref[...], full[:, cols])
        for j in range(8):
            rows = slice(j * 64, (j + 1) * 64)
            v = pre[n % 2, rows]
            sq = v * v
            t = jnp.tanh(v * (0.7978845608 + (0.7978845608 * 0.044715) * sq))
            half = 0.5 + 0.5 * t
            if j == 0:
                act_ref[:, cols] = (v * half).astype(BF)
            slope = half + (0.5 * v) * (1.0 - t * t) * (
                0.7978845608 + (0.7978845608 * 3 * 0.044715) * sq
            )
            up = ups[j][:, cols]
            down[n % 2, rows] = (up.astype(F32) * slope).astype(BF)
        grads = dot(own_ref[0:64, :], down[n % 2]).astype(BF)
        ga_ref[2 * n] = grads[:, :128]
        ga_ref[2 * n + 1] = grads[:, 128:]
        hubs = hubs + dot_nt(grads, adj_ref[:, cols])
    for j in range(4):
        hub_ref[j] = hubs[:, j * 128 : (j + 1) * 128]


GROUPS = ((3, 0), (1, 2))


def back_kernel(swap, part, ints_ref, sb0_ref, sb1_ref, ga_ref, tiles_ref, hub_ref, *rest):
    out, acc = rest[-2:]
    y, z, c = here()
    cc = 1 - c if swap else c
    none = jnp.zeros((64, 128), BF)
    for g, j in enumerate(GROUPS[part]):
        sy = ahead(y, STEPS[j])
        sb_ref = (sb0_ref, sb1_ref)[BACK[j] // 2]
        sb_row = (2 if swap else 0) + BACK[j] % 2
        out[64 + g] = hub_ref[sy].astype(BF)
        for i in range(4):
            sz = ahead(z, STEPS[i])
            s = (sy * 4 + sz) * 2 + cc
            count = ints_ref[8, s]
            acc[0:8] = jnp.zeros((8, 64, 128), F32)
            parts = []
            for k in (0, 2):
                one, two = (ga_ref[ints_ref[4 + k + n, s]] for n in range(2))
                rows = [jnp.concatenate([one, none], axis=1), jnp.concatenate([none, two], axis=1)]
                pair = jnp.concatenate([tiles_ref[s, k], tiles_ref[s, k + 1]], axis=1)
                sums = dot_nt(jnp.concatenate(rows, axis=0), pair)
                parts += [sums[:64], sums[64:]]
            for k in range(4):
                b = jnp.where(k < count, sb_ref[sb_row, sz * 4 + k], 8)
                acc[b] += parts[k]
            n = (g * 4 + i) * 8
            out[n : n + 8] = acc[0:8].astype(BF)


def both(a, b, n):
    return (a[n].astype(F32) + b[n].astype(F32)).astype(BF)


def add_first_kernel(a, b, *outs):
    for g in range(2):
        for r in range(32):
            outs[g][r] = both(a, b, g * 32 + r)
        outs[g][32] = both(a, b, 64 + g)


def add_second_kernel(a, b, *outs):
    hubs = both(a, b, 64)
    for i in range(4):
        for r in range(8):
            outs[i][r] = both(a, b, i * 8 + r)
        outs[i][8] = hubs
    for r in range(32):
        outs[4][r] = both(a, b, 32 + r)
    outs[4][32] = both(a, b, 65)


def four(refs, r):
    return (refs[0][r].astype(F32) + refs[1][r].astype(F32)) + (refs[2][r].astype(F32) + refs[3][r].astype(F32))


def sum_near_kernel(a, b, c, *outs):
    def three(r):
        return (a[r].astype(F32) + (b[r].astype(F32) + c[r].astype(F32))).astype(BF)

    hubs = three(32)
    for i in range(4):
        for r in range(8):
            outs[i][r] = three(i * 8 + r)
        outs[i][8] = hubs


def sum_far_kernel(*refs):
    for r in range(9):
        refs[-1][r] = four(refs[:4], r).astype(BF)


def last_kernel(*rest):
    near, far = rest[:4], rest[4]
    ga_ref, self_ref, ids_ref, out_ref = rest[5:]
    _, z, c = here()

    def halves(v):
        high = v.astype(BF)
        return high, (v - high.astype(F32)).astype(BF)

    lane = lax.broadcasted_iota(jnp.int32, (128, 16), 0)
    which = lax.broadcasted_iota(jnp.int32, (128, 16), 1)
    take = (lane == (z * 2 + c) * 16 + which).astype(F32).astype(BF)
    high, low = halves(four(near, 8) + far[8].astype(F32))
    high, low = halves(dot(high, take) + dot(low, take))
    node = lax.broadcasted_iota(jnp.int32, (1024, 16), 0)
    spread = (node == ids_ref[...]).astype(F32).astype(BF)
    hubs = dot_nt(high, spread) + dot_nt(low, spread)
    for b in range(8):
        cols = slice(b * 128, (b + 1) * 128)
        total = four(near, b) + far[b].astype(F32)
        out_ref[:, cols] = (ga_ref[b].astype(F32) * self_ref[:, cols] + hubs[:, cols] + total).astype(BF)


def call(kernel, name, outs, args, scalars=0, scratch=(), limit=8, out_specs=None, size=MIB, hbm=0, loose=0):
    shapes = [jax.ShapeDtypeStruct(s, d) for s, d in outs]
    return pl.pallas_call(
        kernel,
        out_shape=shapes,
        in_specs=[HB] * hbm + [SM] * scalars + [VM] * (len(args) - scalars - hbm - loose) + [ANY] * loose,
        out_specs=out_specs or [VM] * len(shapes),
        scratch_shapes=list(scratch),
        compiler_params=pltpu.CompilerParams(vmem_limit_bytes=limit * MIB),
        cost_estimate=pl.CostEstimate(flops=0, bytes_accessed=size, transcendentals=0),
        name=name,
    )(*args)


def shards(
    node_feats,
    self_weight,
    hub_ids,
    hub_adjacency,
    send_blocks,
    recv_counts,
    recv_targets,
    recv_tiles,
    weight,
    grad_out,
):
    ids = hub_ids.reshape(1, 16)
    ints = jnp.concatenate(
        [
            jnp.transpose(send_blocks, (0, 2, 1)).reshape(4, 32),
            jnp.transpose(recv_targets, (0, 2, 1)).reshape(4, 32),
            recv_counts,
            jnp.concatenate([ids, ids], axis=1),
        ],
        axis=0,
    )
    tiles = recv_tiles.reshape(32, 4, 128, 128)
    self_row = self_weight.reshape(1, 1024)

    def shape(n):
        return ((n, 64, 128), BF)

    (p0,) = call(prep_kernel, "prep", [shape(9)], (node_feats, ints))
    ps = [p0] + [row_send(p0, 0, k, 0) for k in STEPS[1:]]
    up_late, _ = lax.optimization_barrier((grad_out, p0))
    up_near = [lax.ppermute(up_late, "feat", feat_perm(0, k)) for k in STEPS[1:]]
    (s0,) = call(stack_kernel, "stack", [shape(LIVE)], (*ps, *up_near), loose=3)
    owns = [s0] + [row_send(s0, k, 0, 0) for k in STEPS[1:]]
    swap0 = row_send(s0, 0, 0, 1)
    up, _ = lax.optimization_barrier((grad_out, s0))
    up_far = lax.ppermute(up, "feat", feat_perm(1, 0))
    wt, own = call(
        weight_kernel, "weights", [((512, 512), BF), ((128, 512), BF)],
        (weight, tiles, s0), 0, [pltpu.VMEM((512, 512), BF)], 12, loose=1,
    )
    slots = [
        pltpu.VMEM((9, 64, 128), F32),
        pltpu.VMEM((8, 128), jnp.int32),
        pltpu.SMEM((8, 128), jnp.int32),
        pltpu.SemaphoreType.DMA,
    ]
    listed = ((4, 16), jnp.int32)
    swaps = [swap0, row_send(owns[1], 0, 0, 1)]
    part, sb0 = call(
        functools.partial(agg_kernel, 0), "agg_first", [((8, 64, 128), F32), listed],
        (ints, *owns[:2], *swaps, tiles, hub_adjacency, node_feats, self_row), 1, slots, 16, [VM, SM], 8 * MIB,
    )
    later, _ = lax.optimization_barrier((up_far, own))
    up_two = lax.ppermute(up_far, "feat", feat_perm(0, 2))
    up_one = lax.ppermute(up_far, "feat", feat_perm(0, 1))
    up_three = lax.ppermute(later, "feat", feat_perm(0, 3))
    owns[3], *up_far = lax.optimization_barrier((owns[3], up_far, up_one, up_three, up_two))
    ups = [grad_out, *up_near, *up_far]
    swaps = [row_send(v, 0, 0, 1) for v in owns[2:]]
    agg, sb1 = call(
        functools.partial(agg_kernel, 1), "agg_second", [((64, 1024), BF), listed],
        (ints, *owns[2:], *swaps, tiles, hub_adjacency, part), 1, slots, 16, [VM, SM], 8 * MIB,
    )
    aggs = feat_gather(agg)
    act, ga, hubs = call(
        mid_kernel, "middle", [((64, 1024), BF), shape(8), ((4, 64, 128), F32)], (*aggs, *ups, wt, own, hub_adjacency), 0,
        [
            pltpu.VMEM((512, 1024), BF),
            pltpu.VMEM((2, 512, 256), F32),
            pltpu.VMEM((2, 512, 256), BF),
        ],
        16, None, 16 * MIB,
    )

    def back(swap, part, *tokens):
        (out,) = call(
            functools.partial(back_kernel, swap, part), "back_swap" if swap else "back_own", [shape(66)],
            (ints, sb0, sb1, ga, tiles, hubs, *tokens), 3, [slots[0]], 16, None, 4 * MIB,
            loose=len(tokens),
        )
        return out

    swap0 = back(True, 0)
    came0 = row_send(swap0, 0, 0, 1)
    swap1 = back(True, 1, swap0)
    came1 = row_send(swap1, 0, 0, 1)
    own0 = back(False, 0, swap1)
    *far_sums, near_sum = call(add_second_kernel, "add_first", [shape(9)] * 4 + [shape(LIVE)], (own0, came0), 0, (), 12)
    own1 = back(False, 1, near_sum)
    up_sum, down_sum = call(add_first_kernel, "add_second", [shape(LIVE)] * 2, (own1, came1))
    fars = [far_sums[0]] + [row_send(far_sums[i], 0, STEPS[i], 0) for i in (1, 2, 3)]
    nears = (near_sum, row_send(up_sum, 1, 0, 0), row_send(down_sum, 3, 0, 0))
    zs = call(sum_near_kernel, "sum_near", [shape(9)] * 4, nears)
    (far,) = call(sum_far_kernel, "sum_far", [shape(9)], (*fars, zs[0]), loose=1)
    zs = [zs[0]] + [row_send(zs[i], 0, STEPS[i], 0) for i in (1, 2, 3)]
    far = row_send(far, 2, 0, 0)
    (grad_in,) = call(last_kernel, "last", [((64, 1024), BF)], (*zs, far, ga, self_row, ids))
    return (act, grad_in)


def solution(mesh):
    in_specs = (
        P("feat", "row"),
        P("row"),
        P("row"),
        P(None, "row"),
        P("row", None, None),
        P("row", None),
        P("row", None, None),
        P("row", None, None, None, None),
        P(),
        P("feat", "row"),
    )
    out_specs = (P("feat", "row"), P("feat", "row"))
    return jax.shard_map(shards, mesh=mesh, in_specs=in_specs, out_specs=out_specs, check_vma=False)
```

```python
import functools

import jax
import jax.numpy as jnp
from jax import lax
from jax.experimental import pallas as pl
from jax.experimental.pallas import tpu as pltpu
from jax.sharding import PartitionSpec as P

BF = jnp.bfloat16
F32 = jnp.float32
VM = pl.BlockSpec(memory_space=pltpu.VMEM)
HB = pl.BlockSpec(memory_space=pltpu.HBM)
ANY = pl.BlockSpec(memory_space=pl.ANY)
SM = pl.BlockSpec(memory_space=pltpu.SMEM)
MIB = 1 << 20
STEPS = (0, 1, 3, 2)
BACK = (0, 2, 1, 3)
NY, NZ, NC = 4, 4, 2
EARLY = False
LIVE = 33


def row_perm(dy, dz, dc):
    pairs = []
    for y in range(NY):
        for z in range(NZ):
            for c in range(NC):
                to = (((y + dy) % NY) * NZ + (z + dz) % NZ) * NC + (c + dc) % NC
                pairs.append(((y * NZ + z) * NC + c, to))
    return pairs


def feat_perm(dh, dx):
    return [(h * 4 + x, ((h + dh) % 2) * 4 + (x + dx) % 4) for h in range(2) for x in range(4)]


def row_send(value, dy, dz, dc):
    return lax.ppermute(value, "row", row_perm(dy, dz, dc))


def feat_gather(value):
    across = lax.ppermute(value, "feat", feat_perm(1, 0))
    near = [lax.ppermute(value, "feat", feat_perm(0, k)) for k in STEPS[1:]]
    far = [lax.ppermute(across, "feat", feat_perm(0, k)) for k in STEPS[1:]]
    return [value, *near, across, *far]


def dot(a, b):
    return jnp.dot(a, b, preferred_element_type=F32)


def dot_nt(a, b):
    return lax.dot_general(a, b, (((1,), (1,)), ((), ())), preferred_element_type=F32)


def dot_tn(a, b):
    return lax.dot_general(a, b, (((0,), (0,)), ((), ())), preferred_element_type=F32)


def here():
    me = lax.axis_index("row")
    return lax.div(me, 8), lax.rem(lax.div(me, 2), 4), lax.rem(me, 2)


def ahead(at, step):
    return lax.rem(at + step, 4)


def behind(at, step):
    return lax.rem(at + 4 - step, 4)


def prep_kernel(x_ref, ints_ref, out_ref):
    _, z, c = here()
    window = (z * 2 + c) * 16
    other = (z * 2 + 1 - c) * 16
    for b in range(8):
        out_ref[b] = x_ref[:, b * 128 : (b + 1) * 128]
    rows = lax.broadcasted_iota(jnp.int32, (1024, 16), 0)
    pick = (rows == ints_ref[9:10, 0:16]).astype(F32).astype(BF)
    hubs = dot(x_ref[...], pick).astype(BF)
    lane = lax.broadcasted_iota(jnp.int32, (16, 128), 1)
    which = lax.broadcasted_iota(jnp.int32, (16, 128), 0)
    extra = dot(hubs, (lane == window + which).astype(F32).astype(BF))
    lane = lax.broadcasted_iota(jnp.int32, (4, 128), 1)
    which = lax.broadcasted_iota(jnp.int32, (4, 128), 0)
    place = (lane == other + which).astype(F32)
    ids = dot_tn(ints_ref[0:4, :].astype(F32), place)
    out_ref[8, 0:32, :] = (extra[0:32] + ids).astype(BF)
    out_ref[8, 32:64, :] = extra[32:64].astype(BF)


def stack_kernel(p0, p1, p2, p3, *rest):
    out_ref = rest[-1]
    extra = jnp.zeros((64, 128), F32)
    for i, p in enumerate((p0, p1, p2, p3)):
        out_ref[i * 8 : (i + 1) * 8] = p[0:8]
        extra = extra + p[8].astype(F32)
    out_ref[32] = extra.astype(BF)


def group_rows():
    group = lax.axis_index("feat")
    h, x = lax.div(group, 4), lax.rem(group, 4)
    first = []
    for j in range(8):
        hh = h if j < 4 else 1 - h
        first.append(pl.multiple_of((hh * 4 + behind(x, STEPS[j % 4])) * 64, 64))
    return first


def weight_kernel(w_ref, tiles_ref, _, wt_ref, own_ref, held):
    first = group_rows()
    for j in range(8):
        held[j * 64 : (j + 1) * 64, :] = w_ref[pl.ds(first[j], 64), :]
    held[...] = held[...].T
    for j in range(8):
        wt_ref[j * 64 : (j + 1) * 64, :] = held[pl.ds(first[j], 64), :]
    own_ref[...] = wt_ref[:, 0:128].T


def agg_kernel(part, ints_ref, *rest):
    owns, swaps = rest[:2], rest[2:4]
    if part == 0:
        tiles_ref, adj_ref, x_ref, self_ref, out_ref, sb_ref, acc, ids_v, ids_s, sem = rest[4:]
    else:
        tiles_ref, adj_ref, sum_ref, out_ref, sb_ref, acc, ids_v, ids_s, sem = rest[4:]
    y, z, c = here()
    me = (y * 4 + z) * 2 + c
    row = lax.broadcasted_iota(jnp.int32, (64, 128), 0)
    ids_v[...] = jnp.zeros_like(ids_v)
    for n, src in enumerate((*owns, *swaps)):
        mine = jnp.where(row == me, src[32].astype(F32), 0.0)
        ids_v[n : n + 1, :] = jnp.sum(mine, axis=0, keepdims=True).astype(jnp.int32)
    copy = pltpu.make_async_copy(ids_v, ids_s, sem)
    copy.start()
    side = lax.rem(lax.div(lax.broadcasted_iota(jnp.int32, (64, 128), 1), 16), 2)
    hub = jnp.zeros((64, 1024), F32)
    for n in range(2):
        sy = behind(y, STEPS[part * 2 + n])
        both = jnp.where(side == c, owns[n][32].astype(F32), swaps[n][32].astype(F32)).astype(BF)
        hub = hub + dot(both, adj_ref[pl.ds(pl.multiple_of(sy * 128, 128), 128), :])
    for b in range(8):
        cols = slice(b * 128, (b + 1) * 128)
        if part == 0:
            acc[b] = x_ref[:, cols].astype(F32) * self_ref[:, cols] + hub[:, cols]
        else:
            acc[b] = sum_ref[b] + hub[:, cols]
    acc[8] = jnp.zeros((64, 128), F32)
    copy.wait()
    for m, srcs in enumerate((owns, swaps)):
        cc = 1 - c if m else c
        for n in range(2):
            sy = behind(y, STEPS[part * 2 + n])
            for i in range(4):
                sz = behind(z, STEPS[i])
                s = (sy * 4 + sz) * 2 + cc
                count = ints_ref[8, s]
                parts = []
                for k in range(4):
                    b = ids_s[m * 2 + n, (sz * 2 + 1 - cc) * 16 + k]
                    sb_ref[m * 2 + n, sz * 4 + k] = b
                    parts.append(dot(srcs[n][i * 8 + b], tiles_ref[s, k]))
                for k in range(4):
                    t = jnp.where(k < count, ints_ref[4 + k, s], 8)
                    acc[t] += parts[k]
    if part == 0:
        out_ref[...] = acc[0:8]
    else:
        for b in range(8):
            out_ref[:, b * 128 : (b + 1) * 128] = acc[b].astype(BF)


def mid_kernel(*rest):
    aggs, ups = rest[:8], rest[8:16]
    wt_ref, own_ref, adj_ref, act_ref, ga_ref, hub_ref, full, pre, down = rest[16:]
    hubs = jnp.zeros((64, 512), F32)
    for j in range(8):
        full[j * 64 : (j + 1) * 64, :] = aggs[j][...]
    for n in range(4):
        cols = slice(n * 256, (n + 1) * 256)
        pre[n % 2] = dot(wt_ref[...], full[:, cols])
        for j in range(8):
            rows = slice(j * 64, (j + 1) * 64)
            v = pre[n % 2, rows]
            sq = v * v
            t = jnp.tanh(v * (0.7978845608 + (0.7978845608 * 0.044715) * sq))
            half = 0.5 + 0.5 * t
            if j == 0:
                act_ref[:, cols] = (v * half).astype(BF)
            slope = half + (0.5 * v) * (1.0 - t * t) * (
                0.7978845608 + (0.7978845608 * 3 * 0.044715) * sq
            )
            up = ups[j][:, cols]
            down[n % 2, rows] = (up.astype(F32) * slope).astype(BF)
        grads = dot(own_ref[0:64, :], down[n % 2]).astype(BF)
        ga_ref[2 * n] = grads[:, :128]
        ga_ref[2 * n + 1] = grads[:, 128:]
        hubs = hubs + dot_nt(grads, adj_ref[:, cols])
    for j in range(4):
        hub_ref[j] = hubs[:, j * 128 : (j + 1) * 128]


GROUPS = ((1, 2), (3, 0))


def back_kernel(works, ints_ref, sb0_ref, sb1_ref, ga_ref, tiles_ref, hub_ref, *rest):
    outs, acc = rest[-1 - len(works) : -1], rest[-1]
    y, z, c = here()
    none = jnp.zeros((64, 128), BF)
    for (swap, part), out in zip(works, outs):
        cc = 1 - c if swap else c
        for g, j in enumerate(GROUPS[part]):
            sy = ahead(y, STEPS[j])
            sb_ref = (sb0_ref, sb1_ref)[BACK[j] // 2]
            sb_row = (2 if swap else 0) + BACK[j] % 2
            out[64 + g] = hub_ref[sy].astype(BF)
            for i in range(4):
                sz = ahead(z, STEPS[i])
                s = (sy * 4 + sz) * 2 + cc
                count = ints_ref[8, s]
                acc[0:8] = jnp.zeros((8, 64, 128), F32)
                parts = []
                for k in (0, 2):
                    one, two = (ga_ref[ints_ref[4 + k + n, s]] for n in range(2))
                    rows = [jnp.concatenate([one, none], axis=1), jnp.concatenate([none, two], axis=1)]
                    pair = jnp.concatenate([tiles_ref[s, k], tiles_ref[s, k + 1]], axis=1)
                    sums = dot_nt(jnp.concatenate(rows, axis=0), pair)
                    parts += [sums[:64], sums[64:]]
                for k in range(4):
                    b = jnp.where(k < count, sb_ref[sb_row, sz * 4 + k], 8)
                    acc[b] += parts[k]
                n = (g * 4 + i) * 8
                out[n : n + 8] = acc[0:8].astype(BF)


def both(a, b, n):
    return (a[n].astype(F32) + b[n].astype(F32)).astype(BF)


def add_first_kernel(a, b, *outs):
    for g in range(2):
        for r in range(32):
            outs[g][r] = both(a, b, g * 32 + r)
        outs[g][32] = both(a, b, 64 + g)


def add_second_kernel(a, b, _, *outs):
    hubs = both(a, b, 64)
    for i in range(4):
        for r in range(8):
            outs[i][r] = both(a, b, i * 8 + r)
        outs[i][8] = hubs
    for r in range(32):
        outs[4][r] = both(a, b, 32 + r)
    outs[4][32] = both(a, b, 65)


def four(refs, r):
    return (refs[0][r].astype(F32) + refs[1][r].astype(F32)) + (refs[2][r].astype(F32) + refs[3][r].astype(F32))


def sum_near_kernel(a, b, c, *outs):
    def three(r):
        return (a[r].astype(F32) + (b[r].astype(F32) + c[r].astype(F32))).astype(BF)

    hubs = three(32)
    for i in range(4):
        for r in range(8):
            outs[i][r] = three(i * 8 + r)
        outs[i][8] = hubs


def sum_far_kernel(*refs):
    for r in range(9):
        refs[-1][r] = four(refs[:4], r).astype(BF)


def last_kernel(*rest):
    near, far = rest[:4], rest[4]
    ga_ref, self_ref, ids_ref, out_ref = rest[5:]
    _, z, c = here()

    def halves(v):
        high = v.astype(BF)
        return high, (v - high.astype(F32)).astype(BF)

    lane = lax.broadcasted_iota(jnp.int32, (128, 16), 0)
    which = lax.broadcasted_iota(jnp.int32, (128, 16), 1)
    take = (lane == (z * 2 + c) * 16 + which).astype(F32).astype(BF)
    high, low = halves(four(near, 8) + far[8].astype(F32))
    high, low = halves(dot(high, take) + dot(low, take))
    node = lax.broadcasted_iota(jnp.int32, (1024, 16), 0)
    spread = (node == ids_ref[...]).astype(F32).astype(BF)
    hubs = dot_nt(high, spread) + dot_nt(low, spread)
    for b in range(8):
        cols = slice(b * 128, (b + 1) * 128)
        total = four(near, b) + far[b].astype(F32)
        out_ref[:, cols] = (ga_ref[b].astype(F32) * self_ref[:, cols] + hubs[:, cols] + total).astype(BF)


def call(kernel, name, outs, args, scalars=0, scratch=(), limit=8, out_specs=None, size=MIB, hbm=0, loose=0):
    shapes = [jax.ShapeDtypeStruct(s, d) for s, d in outs]
    return pl.pallas_call(
        kernel,
        out_shape=shapes,
        in_specs=[HB] * hbm + [SM] * scalars + [VM] * (len(args) - scalars - hbm - loose) + [ANY] * loose,
        out_specs=out_specs or [VM] * len(shapes),
        scratch_shapes=list(scratch),
        compiler_params=pltpu.CompilerParams(vmem_limit_bytes=limit * MIB),
        cost_estimate=pl.CostEstimate(flops=0, bytes_accessed=size, transcendentals=0),
        name=name,
    )(*args)


def shards(
    node_feats,
    self_weight,
    hub_ids,
    hub_adjacency,
    send_blocks,
    recv_counts,
    recv_targets,
    recv_tiles,
    weight,
    grad_out,
):
    ids = hub_ids.reshape(1, 16)
    ints = jnp.concatenate(
        [
            jnp.transpose(send_blocks, (0, 2, 1)).reshape(4, 32),
            jnp.transpose(recv_targets, (0, 2, 1)).reshape(4, 32),
            recv_counts,
            jnp.concatenate([ids, ids], axis=1),
        ],
        axis=0,
    )
    tiles = recv_tiles.reshape(32, 4, 128, 128)
    self_row = self_weight.reshape(1, 1024)

    def shape(n):
        return ((n, 64, 128), BF)

    (p0,) = call(prep_kernel, "prep", [shape(9)], (node_feats, ints))
    ps = [p0] + [row_send(p0, 0, k, 0) for k in STEPS[1:]]
    up_late, _ = lax.optimization_barrier((grad_out, p0))
    up_near = [lax.ppermute(up_late, "feat", feat_perm(0, k)) for k in STEPS[1:]]
    (s0,) = call(stack_kernel, "stack", [shape(LIVE)], (*ps, *up_near), loose=3)
    owns = [s0] + [row_send(s0, k, 0, 0) for k in STEPS[1:]]
    swap0 = row_send(s0, 0, 0, 1)
    up, _ = lax.optimization_barrier((grad_out, s0))
    up_far = lax.ppermute(up, "feat", feat_perm(1, 0))
    wt, own = call(
        weight_kernel, "weights", [((512, 512), BF), ((128, 512), BF)],
        (weight, tiles, s0), 0, [pltpu.VMEM((512, 512), BF)], 12, loose=1,
    )
    slots = [
        pltpu.VMEM((9, 64, 128), F32),
        pltpu.VMEM((8, 128), jnp.int32),
        pltpu.SMEM((8, 128), jnp.int32),
        pltpu.SemaphoreType.DMA,
    ]
    listed = ((4, 16), jnp.int32)
    swaps = [swap0, row_send(owns[1], 0, 0, 1)]
    part, sb0 = call(
        functools.partial(agg_kernel, 0), "agg_first", [((8, 64, 128), F32), listed],
        (ints, *owns[:2], *swaps, tiles, hub_adjacency, node_feats, self_row), 1, slots, 16, [VM, SM], 8 * MIB,
    )
    later, _ = lax.optimization_barrier((up_far, own))
    up_two = lax.ppermute(up_far, "feat", feat_perm(0, 2))
    up_one = lax.ppermute(up_far, "feat", feat_perm(0, 1))
    up_three = lax.ppermute(later, "feat", feat_perm(0, 3))
    owns[3], *up_far = lax.optimization_barrier((owns[3], up_far, up_one, up_three, up_two))
    ups = [grad_out, *up_near, *up_far]
    swaps = [row_send(v, 0, 0, 1) for v in owns[2:]]
    agg, sb1 = call(
        functools.partial(agg_kernel, 1), "agg_second", [((64, 1024), BF), listed],
        (ints, *owns[2:], *swaps, tiles, hub_adjacency, part), 1, slots, 16, [VM, SM], 8 * MIB,
    )
    aggs = feat_gather(agg)
    act, ga, hubs = call(
        mid_kernel, "middle", [((64, 1024), BF), shape(8), ((4, 64, 128), F32)], (*aggs, *ups, wt, own, hub_adjacency), 0,
        [
            pltpu.VMEM((512, 1024), BF),
            pltpu.VMEM((2, 512, 256), F32),
            pltpu.VMEM((2, 512, 256), BF),
        ],
        16, None, 16 * MIB,
    )

    def back(name, works, *tokens):
        return call(
            functools.partial(back_kernel, works), name, [shape(66)] * len(works),
            (ints, sb0, sb1, ga, tiles, hubs, *tokens), 3, [slots[0]], 16, None, 4 * MIB,
            loose=len(tokens),
        )

    (away0,) = back("back_first", ((True, 0),))
    came0 = row_send(away0, 0, 0, 1)
    away1, own0, own1 = back("back_rest", ((True, 1), (False, 0), (False, 1)), away0)
    came1 = row_send(away1, 0, 0, 1)
    up_sum, down_sum = call(add_first_kernel, "add_first", [shape(LIVE)] * 2, (own0, came0))
    *far_sums, near_sum = call(
        add_second_kernel, "add_second", [shape(9)] * 4 + [shape(LIVE)], (own1, came1, up_sum), 0, (), 12, loose=1
    )
    fars = [far_sums[0]] + [row_send(far_sums[i], 0, STEPS[i], 0) for i in (1, 2, 3)]
    nears = (near_sum, row_send(up_sum, 1, 0, 0), row_send(down_sum, 3, 0, 0))
    zs = call(sum_near_kernel, "sum_near", [shape(9)] * 4, nears)
    zs = [zs[0]] + [row_send(zs[i], 0, STEPS[i], 0) for i in (1, 2, 3)]
    (far,) = call(sum_far_kernel, "sum_far", [shape(9)], (*fars, zs[1]), loose=1)
    far = row_send(far, 2, 0, 0)
    (grad_in,) = call(last_kernel, "last", [((64, 1024), BF)], (*zs, far, ga, self_row, ids))
    return (act, grad_in)


def solution(mesh):
    in_specs = (
        P("feat", "row"),
        P("row"),
        P("row"),
        P(None, "row"),
        P("row", None, None),
        P("row", None),
        P("row", None, None),
        P("row", None, None, None, None),
        P(),
        P("feat", "row"),
    )
    out_specs = (P("feat", "row"), P("feat", "row"))
    return jax.shard_map(shards, mesh=mesh, in_specs=in_specs, out_specs=out_specs, check_vma=False)
```
